256 devices in a mesh: sec: 2 (over y_lo), ri: 64 (over z, x, core), ao: 2 (over y_hi).
Axes of the slice: x: 4, y: 4 (y_hi: 2, y_lo: 2; y = y_hi * 2 + y_lo), z: 8, core: 2. Of those that a mesh axis runs over, the one named last changes fastest.
Arguments:
- coulomb_band: bfloat16 [16384, 768], P('ri'), may hold values from -0.21875 to 0.21875
- band_mask: int32 [256, 12], P('ri'), may hold values from 0 to 1, as said below
- dielectric: bfloat16 [2, 16384, 1024], P('sec', 'ri', 'ao'), may hold values from -6 to 6
- three_centre: bfloat16 [16384, 128, 128], P('ri', 'sec'), may hold values from -0.099121094 to 0.099121094
- centre_mask: int32 [256], P('ri'), may hold values 0 or 1
- greens: bfloat16 [2, 512, 512], P('sec', 'ao'), may hold values from -0.5 to 0.5
- tile_map: int32 [64, 1], replicated, may hold values from 0 to 3
- batch_order: int32 [2, 64], replicated, may hold values from 0 to 63, each once within a row
Outputs:
- self_energy: float32 [2, 512, 512], P('sec', ('ri', 'ao'))
The draws below stay inside these ranges and needn't reach their ends.
Inputs may be any that keep to these rules, and one draw needn't show every extreme that they name: `band_mask`: in every row of tiles, the tile on the block's diagonal within the lower neighbour's 256 columns and within the upper neighbour's 256 columns is 1. `batch_order`: each row names every block once. `tile_map`: every AO tile is the tile of some block.
All inputs are finite; a program needn't handle non-finite values. No bound on the sum of `centre_mask` on one device may be relied on, other than what follows from the above.
Results may differ from the reference program's by a relative error of at most 0.0049.
Values may be sent and summed in bfloat16 or wider, within the bound.
No kernel may reach another device: no remote copies, remote signals or barrier semaphores. Data moves between devices by JAX's collectives and lax.ppermute only.
A program may use at most 192 MiB of HBM per device.

```python
import jax
import jax.numpy as jnp
from jax import lax

RT = 256
TA = 128
QB = 1024
NTILE = 4
NT = 2
NRI = 16384
NA = 512
N_RI = 64


def draw_band_mask(key, part):
    key = jax.random.fold_in(key, 11)
    tile_rows = NRI // 64
    tile_cols = 3 * RT // 64
    per_block = RT // 64
    base = (jax.random.randint(key, (tile_rows, tile_cols), 0, 4) < 3).astype(jnp.int32)
    row_ids = jnp.arange(tile_rows, dtype=jnp.int32)[:, None]
    col_ids = jnp.arange(tile_cols, dtype=jnp.int32)[None, :]
    outside = (col_ids < per_block) | (col_ids >= 2 * per_block)
    forced = outside & (col_ids % per_block == row_ids % per_block)
    return jnp.where(forced, 1, base).astype(jnp.int32)


def touch_ends(array, stream_key, smallest, largest):
    index_at = [jax.random.randint(jax.random.fold_in(stream_key, axis), (), 0, length) for axis, length in enumerate(array.shape)]
    main_axis = array.shape.index(max(array.shape))
    neighbour = index_at[:main_axis] + [(index_at[main_axis] + 1) % array.shape[main_axis]] + index_at[main_axis + 1:]
    return array.at[tuple(index_at)].set(smallest).at[tuple(neighbour)].set(largest)


def level_of(stream_key, shape, split, smallest, largest):
    def one(position, blocks):
        steps = jax.random.uniform(jax.random.fold_in(jax.random.fold_in(stream_key, 6), position), (blocks,), jnp.float32, smallest / len(split), largest / len(split))
        return jnp.repeat(jnp.exp(steps), shape[position] // blocks).reshape((-1,) + (1,) * (len(shape) - position - 1))

    level = one(*split[0])
    for cut in split[1:]:
        level = level * one(*cut)
    return level


def different_ones(own_key, rows, amount, top, lift):
    order = jax.random.permutation(jax.random.fold_in(own_key, 1), amount)
    favour = order
    for power in range(3):
        favour = favour * favour // amount
    favour = favour * lift // amount
    lots = jax.random.randint(jax.random.fold_in(own_key, 2), (rows, amount), 0, 4096) + favour
    fixed_rows = jax.random.permutation(jax.random.fold_in(own_key, 3), rows)[jnp.arange(amount) % rows]
    lots = jnp.where(jnp.arange(rows)[:, None] == fixed_rows[None, :], 1 << 14, lots)
    score = lots * amount + jnp.arange(amount)
    return lax.top_k(score.astype(jnp.int32), top)[1].astype(jnp.int32)


def normal_values(own_key, shape, scale, bound, shards=(), kind=jnp.bfloat16):
    drawn = jax.random.normal(own_key, shape, jnp.float32) * scale
    if len(shards) > 0:
        drawn = level_of(own_key, shape, shards, -0.22, 0.18) * drawn
    return jnp.clip(drawn, min=-bound, max=bound).astype(kind)


def setup_inputs(seed: int = 0) -> dict:
    arg_keys = jax.random.split(jax.random.key(seed), 9)
    return {
        "coulomb_band": normal_values(arg_keys[0], (NRI, 3 * RT), (3 * RT) ** -0.5, 0.21875, ((0, 64),)),
        "band_mask": draw_band_mask(jax.random.fold_in(arg_keys[8], 71), 0),
        "dielectric": normal_values(arg_keys[2], (NT, NRI, QB), 1.0, 6.0, ((0, 2), (1, 64), (2, 2))),
        "three_centre": normal_values(arg_keys[3], (NRI, TA, TA), (3.0 / (RT * TA) ** 0.5), 0.099121094, ((0, 64), (1, 2))),
        "centre_mask": touch_ends((jax.random.randint(arg_keys[4], (NRI // 64,), 0, 3) < 2).astype(jnp.int32), jax.random.fold_in(arg_keys[4], 1), 0, 1),
        "greens": normal_values(arg_keys[5], (NT, NA, NA), TA ** -0.5, 0.5, ((0, 2), (1, 2))),
        "tile_map": different_ones(arg_keys[6], N_RI, NTILE, 1, 4096),
        "batch_order": jax.vmap(lambda own: jax.random.permutation(own, N_RI))(jax.random.split(arg_keys[7], NT)).reshape((NT, N_RI)).astype(jnp.int32),
    }


def reference(coulomb_band, band_mask, dielectric, three_centre, centre_mask, greens, tile_map, batch_order):
    mask_full = jnp.repeat(jnp.repeat(band_mask, 64, axis=0), 64, axis=1).astype(jnp.bfloat16)
    band = (coulomb_band * mask_full).reshape(N_RI, RT, 3 * RT)
    keep = jnp.repeat(centre_mask, 64).astype(jnp.bfloat16)
    centre = three_centre * keep[:, None, None]
    flat = centre.reshape(N_RI, RT, TA * TA)
    tiles = tile_map[:, 0].astype(jnp.int32)
    results = []
    for tpoint in range(NT):
        factor = dielectric[tpoint].reshape(N_RI, RT, QB)
        stacked = jnp.concatenate([jnp.roll(factor, 1, axis=0), factor, jnp.roll(factor, -1, axis=0)], axis=1)
        screened = jnp.einsum("apr,arc->apc", band.astype(jnp.float32), stacked.astype(jnp.float32)).astype(jnp.bfloat16)
        green_now = greens[tpoint]
        total = jnp.zeros((NA, NA), jnp.float32)
        for slot in range(QB // RT):
            owner = batch_order[tpoint, slot].astype(jnp.int32)
            other_tile = tiles[owner].astype(jnp.int32)
            fetched = flat[owner].reshape(RT, TA, TA)
            columns = screened[:, :, slot * RT:(slot + 1) * RT]

            def one_block(carry, inputs):
                cols_a, flat_a, tile_a = inputs
                s_block = jnp.dot(cols_a.T, flat_a, preferred_element_type=jnp.float32).astype(jnp.bfloat16)
                row0 = (tile_a * TA).astype(jnp.int32)
                col0 = (other_tile * TA).astype(jnp.int32)
                g_tile = lax.dynamic_slice(green_now, (row0, col0), (TA, TA))
                y_block = jnp.dot(s_block.reshape(RT * TA, TA), g_tile, preferred_element_type=jnp.float32)
                y_block = y_block.astype(jnp.bfloat16).reshape(RT, TA, TA)
                part = jnp.einsum("qms,qns->mn", y_block.astype(jnp.float32), fetched.astype(jnp.float32))
                current = lax.dynamic_slice(carry, (row0, col0), (TA, TA))
                return lax.dynamic_update_slice(carry, current - part, (row0, col0)), None

            total, unused = lax.scan(one_block, total, (columns, flat, tiles))
        results.append(total)
    return jnp.stack(results, axis=0)
```

```python
import jax
import jax.numpy as jnp
from jax import lax
from jax.experimental import pallas as pl
from jax.experimental.pallas import tpu as pltpu
from jax.sharding import Mesh, PartitionSpec as P

NZ, NX, NC = 8, 4, 2
CHIPS = NZ * NX
BF = jnp.bfloat16
F32 = jnp.float32


def shift(value, axis, by):
    n = lax.axis_size(axis)
    return lax.ppermute(value, axis, [(i, (i + by) % n) for i in range(n)])


def y_kernel(wt_ref, g_ref, lo_ref, hi_ref, y_ref, m_scr, y_scr):
    half = lo_ref.shape[0] * lo_ref.shape[1]
    group = lo_ref.shape[1]
    rows = 2 * lo_ref.shape[0]
    lane = lo_ref.shape[2]
    m_scr[0:half, :] = lo_ref[...].astype(F32).reshape(half, lane)
    m_scr[half : 2 * half, :] = hi_ref[...].astype(F32).reshape(half, lane)
    wt = wt_ref[...]
    g = g_ref[...]
    for mu in range(0, group, 2):
        m = jnp.concatenate(
            [m_scr[pl.ds(mu + i, rows, stride=group), :].astype(BF) for i in range(2)], axis=1
        )
        s = jnp.dot(wt, m, preferred_element_type=F32).astype(BF)
        y = jnp.dot(s, g, preferred_element_type=F32)
        for i in range(2):
            y_scr[pl.ds(mu + i, rows, stride=group), :] = y[:, i * lane : (i + 1) * lane]
    y_ref[...] = y_scr[...].astype(BF).reshape(rows, group, lane)


def y_part(wt, g2, lo, hi, hi_block):
    rows, mus, lane = wt.shape[0], lo.shape[1], lo.shape[2]
    group = 16
    return pl.pallas_call(
        y_kernel,
        grid=(mus // group,),
        in_specs=[
            pl.BlockSpec((rows, rows), lambda i: (0, 0)),
            pl.BlockSpec((2 * lane, 2 * lane), lambda i: (0, 0)),
            pl.BlockSpec((rows // 2, group, lane), lambda i: (0, i, 0)),
            pl.BlockSpec((rows // 2, group, lane), lambda i: (hi_block, i, 0)),
        ],
        out_specs=pl.BlockSpec((rows, group, lane), lambda i: (0, i, 0)),
        out_shape=jax.ShapeDtypeStruct((rows, mus, lane), BF),
        scratch_shapes=[pltpu.VMEM((rows * group, lane), F32), pltpu.VMEM((rows * group, lane), F32)],
        compiler_params=pltpu.CompilerParams(vmem_limit_bytes=32 << 20),
        cost_estimate=pl.CostEstimate(
            flops=2 * rows * rows * mus * lane * 3 // 2, bytes_accessed=4 * rows * mus * lane, transcendentals=0
        ),
        name="y_part",
    )(wt, g2, lo, hi)


def contract_kernel(parts, per, tab_ref, *refs):
    out_ref = refs[-1]
    f_ref = refs[-2]
    q = refs[0].shape[0]

    @pl.when(pl.program_id(0) == 0)
    def _():
        out_ref[...] = jnp.zeros_like(out_ref)

    acc = out_ref[...]
    for piece in range(per):
        for i in range(0, q, 2):
            lhs = jnp.concatenate(
                [
                    jnp.concatenate([refs[part * per + piece][i], refs[part * per + piece][i + 1]], axis=1)
                    for part in range(parts)
                ],
                axis=0,
            )
            rhs = jnp.concatenate([f_ref[piece * q + i], f_ref[piece * q + i + 1]], axis=1)
            acc += lax.dot_general(lhs, rhs, (((1,), (1,)), ((), ())), preferred_element_type=F32)
    out_ref[...] = acc


def contract(ys, fetched, table, q):
    parts = len(ys)
    pieces = fetched.shape[0] // q
    per = min(4, pieces)
    mus, lane = ys[0].shape[1], ys[0].shape[2]
    nus = fetched.shape[1]

    def y_spec(piece):
        return pl.BlockSpec((q, mus, lane), lambda i, tab: (tab[i * per + piece], 0, 0))

    specs = [y_spec(piece) for _ in range(parts) for piece in range(per)]
    specs.append(pl.BlockSpec((per * q, nus, lane), lambda i, tab: (i, 0, 0)))
    return pl.pallas_call(
        lambda *refs: contract_kernel(parts, per, *refs),
        grid_spec=pltpu.PrefetchScalarGridSpec(
            num_scalar_prefetch=1,
            grid=(pieces // per,),
            in_specs=specs,
            out_specs=pl.BlockSpec((parts * mus, nus), lambda i, tab: (0, 0)),
        ),
        out_shape=jax.ShapeDtypeStruct((parts * mus, nus), F32),
        compiler_params=pltpu.CompilerParams(vmem_limit_bytes=32 << 20),
        cost_estimate=pl.CostEstimate(
            flops=2 * parts * mus * nus * lane * q * pieces,
            bytes_accessed=2 * q * pieces * lane * (parts * mus + nus),
            transcendentals=0,
        ),
        name="contract",
    )(table, *[ys[part] for part in range(parts) for _ in range(per)], fetched)


def pick_kernel(tab_ref, in_ref, out_ref):
    out_ref[...] = in_ref[...]


def pick(buffer, table, count):
    block = (1,) + buffer.shape[1:]
    zeros = (0,) * (buffer.ndim - 1)
    return pl.pallas_call(
        pick_kernel,
        grid_spec=pltpu.PrefetchScalarGridSpec(
            num_scalar_prefetch=1,
            grid=(count,),
            in_specs=[pl.BlockSpec(block, lambda i, tab: (tab[i],) + zeros)],
            out_specs=pl.BlockSpec(block, lambda i, tab: (i,) + zeros),
        ),
        out_shape=jax.ShapeDtypeStruct((count,) + buffer.shape[1:], buffer.dtype),
        name="pick",
    )(table, buffer)


def body(
    coulomb_band, band_mask, dielectric, three_centre, centre_mask, greens, tile_map, batch_order
):
    rows = coulomb_band.shape[0]
    mus = three_centre.shape[1]
    width = three_centre.shape[2]
    z, x, c = lax.axis_index("z"), lax.axis_index("x"), lax.axis_index("core")
    s, h = lax.axis_index("sec"), lax.axis_index("ao")
    ri = (z * NX + x) * NC + c
    tiles = tile_map[:, 0]
    keep = jnp.repeat(centre_mask, rows // centre_mask.shape[0]).astype(BF)

    owners = batch_order[:, :4]
    chips, cores = owners // NC, owners % NC

    half_rows = rows // 2
    send = lax.dynamic_slice_in_dim(three_centre, h * half_rows, half_rows, axis=0)
    send = send * lax.dynamic_slice_in_dim(keep, h * half_rows, half_rows)[:, None, None]
    spread = lax.all_to_all(send, ("z", "x"), 0, 0, tiled=True)
    q = half_rows // CHIPS
    spread = spread.reshape(CHIPS, q, mus, width)

    ring = [(i, (i + 1) % (CHIPS * NC)) for i in range(CHIPS * NC)]
    back = [(j, i) for i, j in ring]
    own_x = dielectric[0]
    before = lax.ppermute(own_x, ("z", "x", "core"), ring)
    after = lax.ppermute(own_x, ("z", "x", "core"), back)
    mask_full = jnp.repeat(jnp.repeat(band_mask, 64, axis=0), 64, axis=1).astype(BF)
    band = coulomb_band * mask_full
    stacked = jnp.concatenate([before, own_x, after], axis=0)
    wt = lax.dot_general(stacked, band, (((0,), (1,)), ((), ())), preferred_element_type=F32).astype(BF)
    wt = wt * keep[None, :]
    wt_own = lax.dynamic_slice_in_dim(wt, c * rows, rows, axis=0)
    wt_oth = shift(lax.dynamic_slice_in_dim(wt, (1 - c) * rows, rows, axis=0), "core", 1)

    g_other = shift(greens[0], "ao", 1)
    green = jnp.concatenate(
        [jnp.where(h == 0, greens[0], g_other), jnp.where(h == 0, g_other, greens[0])], axis=0
    )
    my_owner = owners[s, 2 * h + c]
    col0 = tiles[my_owner] * width
    tile_own, tile_oth = tiles[ri], tiles[ri + 1 - 2 * c]

    def g_pair(tile):
        g = lax.dynamic_slice(green, (tile * width, col0), (width, width))
        zero = jnp.zeros_like(g)
        return jnp.concatenate(
            [jnp.concatenate([g, zero], axis=1), jnp.concatenate([zero, g], axis=1)], axis=0
        )

    g_own, g_oth = g_pair(tile_own), g_pair(tile_oth)

    along_y = (0, 2, 1, 3)
    quad = [(along_y[i], along_y[(i + 1) % 4]) for i in range(4)]
    quad_back = [(j, i) for i, j in quad]
    m_core = shift(three_centre, "core", 1)
    o_lo = lax.ppermute(three_centre[:half_rows], ("sec", "ao"), quad)
    o_hi = lax.ppermute(three_centre[half_rows:], ("sec", "ao"), quad_back)
    oc_lo, oc_hi = shift(o_lo, "core", 1), shift(o_hi, "core", 1)
    ys = [
        y_part(wt_own, g_own, three_centre, three_centre, 1),
        y_part(wt_oth, g_oth, m_core, m_core, 1),
        y_part(wt_own, g_own, o_lo, o_hi, 0),
        y_part(wt_oth, g_oth, oc_lo, oc_hi, 0),
    ]

    def flows(core):
        return jnp.stack([chips[t, 2 * hh + core] for t in range(2) for hh in range(2)]).astype(jnp.int32)

    def flow_cores(core):
        return jnp.stack([cores[t, 2 * hh + core] for t in range(2) for hh in range(2)])

    given = shift(pick(spread, flows(1 - c), 4), "core", 1)
    kept = pick(spread, flows(c), 4)
    mine = jnp.where((flow_cores(c) == c)[:, None, None, None], kept, given)
    quads = lax.all_to_all(mine, ("sec", "ao"), 0, 0, tiled=True)
    halves = jnp.transpose(quads.reshape(2, 2, q, mus, width), (1, 2, 0, 3, 4)).reshape(2, q, 2 * mus, width)
    piece_a, piece_b = halves[0], halves[1]

    totals = []

    rel_x = (0, 1, 2, 3)
    chunk = jnp.concatenate([piece_a] + [shift(piece_a, "x", d) for d in rel_x[1:]], axis=0)
    xs_a = [(x - d) % NX for d in rel_x]

    def add_a(value, offset, first, count):
        table = jnp.stack([((z - offset) % NZ) * NX + xs_a[first + i] for i in range(count)]).astype(jnp.int32)
        totals.append(contract(ys, value, table, q))

    add_a(chunk, 0, 0, 4)
    up, down = chunk, chunk
    for step in range(1, NZ // 2):
        up, down = shift(up, "z", 1), shift(down, "z", -1)
        add_a(up, step, 0, 4)
        add_a(down, -step, 0, 4)
    part = chunk.shape[0] // 2
    add_a(shift(up[:part], "z", 1), NZ // 2, 0, 2)
    add_a(shift(down[part:], "z", -1), NZ // 2, 2, 2)

    pieces, rel_z = [piece_b], [0]
    up, down = piece_b, piece_b
    for step in range(1, NZ // 2):
        up, down = shift(up, "z", 1), shift(down, "z", -1)
        pieces += [up, down]
        rel_z += [step, -step]
    pieces.append(shift(up, "z", 1))
    rel_z.append(NZ // 2)
    chunk = jnp.concatenate(pieces, axis=0)
    zs_b = [(z - d) % NZ for d in rel_z]

    def add_b(value, offset, first, count):
        table = jnp.stack(
            [CHIPS + zs_b[first + i] * NX + (x - offset) % NX for i in range(count)]
        ).astype(jnp.int32)
        totals.append(contract(ys, value, table, q))

    add_b(chunk, 0, 0, 8)
    up, down = shift(chunk, "x", 1), shift(chunk, "x", -1)
    add_b(up, 1, 0, 8)
    add_b(down, -1, 0, 8)
    part = chunk.shape[0] // 2
    add_b(shift(up[:part], "x", 1), 2, 0, 4)
    add_b(shift(down[part:], "x", -1), 2, 4, 4)

    total = -sum(totals)
    places = jnp.arange(8, dtype=jnp.int32)
    partial = jnp.zeros((8, mus, width), F32)
    for part, (tile, half) in enumerate(
        ((tile_own, s), (tile_oth, s), (tile_own, 1 - s), (tile_oth, 1 - s))
    ):
        here = (places == 2 * tile + half)[:, None, None]
        partial = partial + jnp.where(here, total[part * mus : (part + 1) * mus][None], 0.0)
    partial = partial.reshape(8 * mus, width)
    moved = lax.all_to_all(partial, ("z", "x", "core", "ao"), 0, 0, tiled=True)
    own_rows = partial.shape[0] // (CHIPS * NC * 2)
    summed = jnp.sum(moved.reshape(CHIPS, NC, 2, own_rows, width), axis=0)
    out = jnp.zeros((own_rows, 4, width), F32)
    col_places = jnp.arange(4, dtype=jnp.int32)
    for hh in range(2):
        for cc in range(2):
            there = (col_places == tiles[owners[s, 2 * hh + cc]])[None, :, None]
            out = out + jnp.where(there, summed[cc, hh][:, None, :], 0.0)
    return out.reshape(1, own_rows, 4 * width)


def solution(mesh):
    devices = mesh.devices.reshape(2, NZ, NX, NC, 2)
    split = Mesh(devices, ("sec", "z", "x", "core", "ao"))
    ri = ("z", "x", "core")
    placed = (
        P(ri, None),
        P(ri, None),
        P("sec", ri, "ao"),
        P(ri, "sec", None),
        P(ri),
        P("sec", "ao", None),
        P(),
        P(),
    )
    return jax.shard_map(
        body, mesh=split, in_specs=placed, out_specs=P("sec", ri + ("ao",), None), check_vma=False
    )
```

```python
import jax
import jax.numpy as jnp
from jax import lax
from jax.experimental import pallas as pl
from jax.experimental.pallas import tpu as pltpu
from jax.sharding import Mesh, PartitionSpec as P

NZ, NX, NC = 8, 4, 2
CHIPS = NZ * NX
VMEM = 60 << 20
BF = jnp.bfloat16
F32 = jnp.float32


def shift(value, axis, by):
    n = lax.axis_size(axis)
    return lax.ppermute(value, axis, [(i, (i + by) % n) for i in range(n)])


def along_y():
    pairs = []
    for y in range(4):
        for core, to in ((0, (y + 1) % 4), (1, (y + 3) % 4)):
            pairs.append(tuple(((p % 2) * NC + core) * 2 + p // 2 for p in (y, to)))
    return pairs


def y_kernel(wt_ref, g_ref, m_ref, y_ref, m_scr, y_scr):
    rows, group, lane = m_ref.shape
    m_scr[...] = m_ref[...].astype(F32).reshape(rows * group, lane)
    wt = wt_ref[...]
    g = g_ref[0]
    for mu in range(0, group, 2):
        m = jnp.concatenate(
            [m_scr[pl.ds(mu + i, rows, stride=group), :].astype(BF) for i in range(2)], axis=1
        )
        s = jnp.dot(wt, m, preferred_element_type=F32).astype(BF)
        y = jnp.dot(s, g, preferred_element_type=F32)
        for i in range(2):
            y_scr[pl.ds(mu + i, rows, stride=group), :] = y[:, i * lane : (i + 1) * lane]
    y_ref[...] = y_scr[...].astype(BF).reshape(rows, group, lane)


def y_part(before, part, wt, g2, block):
    rows, mus, lane = block.shape
    group = 16
    steps = mus // group
    specs = [
        pl.BlockSpec((rows, rows), lambda i: (0, 0)),
        pl.BlockSpec((1, 2 * lane, 2 * lane), lambda i: (part % 2, 0, 0)),
        pl.BlockSpec((rows, group, lane), lambda i: (0, i, 0)),
    ]
    args = [wt, g2, block]
    aliases = {}
    kernel = y_kernel
    if before is not None:
        specs.append(pl.BlockSpec(memory_space=pl.ANY))
        args.append(before)
        aliases = {3: 0}

        def kernel(w, g, m, unused, *rest):
            y_kernel(w, g, m, *rest)

    return pl.pallas_call(
        kernel,
        grid=(steps,),
        in_specs=specs,
        out_specs=pl.BlockSpec((rows, group, lane), lambda i: (0, part * steps + i, 0)),
        out_shape=jax.ShapeDtypeStruct((rows, 4 * mus, lane), BF),
        input_output_aliases=aliases,
        scratch_shapes=[pltpu.VMEM((rows * group, lane), F32), pltpu.VMEM((rows * group, lane), F32)],
        compiler_params=pltpu.CompilerParams(vmem_limit_bytes=VMEM),
        cost_estimate=pl.CostEstimate(flops=40 * rows * rows * mus * lane, bytes_accessed=80 * rows * mus * lane, transcendentals=0),
        name="y_part",
    )(*args)


def after(value, *others, weight=0):
    return pl.pallas_call(
        lambda *refs: None,
        in_specs=[pl.BlockSpec(memory_space=pl.ANY)] * (1 + len(others)),
        out_specs=pl.BlockSpec(memory_space=pl.ANY),
        out_shape=jax.ShapeDtypeStruct(value.shape, value.dtype),
        input_output_aliases={0: 0},
        compiler_params=pltpu.CompilerParams(vmem_limit_bytes=VMEM),
        cost_estimate=pl.CostEstimate(
            flops=weight * 1000000000, bytes_accessed=weight * 3000000, transcendentals=0
        ),
        name="after",
    )(value, *others)


def contract_kernel(counts, more, tab_ref, *refs):
    out_ref = refs[-1]
    pieces = sum(counts)
    q = refs[0].shape[0]

    @pl.when(pl.program_id(0) == 0)
    def _():
        out_ref[...] = refs[-2][...] if more else jnp.zeros_like(out_ref)

    acc = out_ref[...]
    place = 0
    for source, count in enumerate(counts):
        f_ref = refs[pieces + source]
        for piece in range(count):
            y_ref = refs[place]
            place += 1
            for i in range(0, q, 2):
                lhs = jnp.concatenate([y_ref[i], y_ref[i + 1]], axis=1)
                rhs = jnp.concatenate([f_ref[piece * q + i], f_ref[piece * q + i + 1]], axis=1)
                acc += lax.dot_general(lhs, rhs, (((1,), (1,)), ((), ())), preferred_element_type=F32)
    out_ref[...] = acc


def contract(before, ys, table, chunks, q, steps=2):
    values = [value for value, _ in chunks]
    counts = [value.shape[0] // q // steps for value in values]
    per = sum(counts)
    rows, lane = ys.shape[1], ys.shape[2]
    nus = values[0].shape[1]

    def y_spec(start, count):
        return pl.BlockSpec((q, rows, lane), lambda i, tab: (tab[start + i * count], 0, 0))

    specs = [
        y_spec(start + piece, count)
        for (_, start), count in zip(chunks, counts)
        for piece in range(count)
    ]
    specs += [pl.BlockSpec((count * q, nus, lane), lambda i, tab: (i, 0, 0)) for count in counts]
    args = [table] + [ys] * per + values
    if before is not None:
        specs.append(pl.BlockSpec((rows, nus), lambda i, tab: (0, 0)))
        args.append(before)
    return pl.pallas_call(
        lambda *refs: contract_kernel(counts, before is not None, *refs),
        grid_spec=pltpu.PrefetchScalarGridSpec(
            num_scalar_prefetch=1,
            grid=(steps,),
            in_specs=specs,
            out_specs=pl.BlockSpec((rows, nus), lambda i, tab: (0, 0)),
        ),
        out_shape=jax.ShapeDtypeStruct((rows, nus), F32),
        compiler_params=pltpu.CompilerParams(vmem_limit_bytes=VMEM),
        cost_estimate=pl.CostEstimate(
            flops=2 * rows * nus * lane * q * per * steps,
            bytes_accessed=2 * q * per * steps * lane * (rows + nus),
            transcendentals=0,
        ),
        name="contract",
    )(*args)


def pick(buffer, table, count, others):
    block = (1,) + buffer.shape[1:]
    zeros = (0,) * (buffer.ndim - 1)

    def spec(i):
        return pl.BlockSpec(block, lambda j, tab: (tab[i],) + zeros)

    def kernel(tab_ref, *refs):
        for i in range(count):
            refs[-1][i] = refs[i][0]

    return pl.pallas_call(
        kernel,
        grid_spec=pltpu.PrefetchScalarGridSpec(
            num_scalar_prefetch=1,
            grid=(1,),
            in_specs=[spec(i) for i in range(count)] + [pl.BlockSpec(memory_space=pl.ANY)] * len(others),
            out_specs=pl.BlockSpec((count,) + buffer.shape[1:], lambda j, tab: (0,) + zeros),
        ),
        out_shape=jax.ShapeDtypeStruct((count,) + buffer.shape[1:], buffer.dtype),
        compiler_params=pltpu.CompilerParams(vmem_limit_bytes=VMEM),
        cost_estimate=pl.CostEstimate(flops=1000, bytes_accessed=1000, transcendentals=0),
        name="pick",
    )(table, *([buffer] * count), *others)


def masked_rows(value, half, mask):
    groups = mask.shape[0]
    steps = 4
    rows = value.shape[0] // 2
    step_rows = rows // steps
    table = jnp.concatenate([half.reshape(1), mask]).astype(jnp.int32)
    block = (step_rows,) + value.shape[1:]

    def kernel(tab_ref, in_ref, out_ref):
        row = tab_ref[0] * rows + pl.program_id(0) * step_rows
        keep = tab_ref[1 + row // (value.shape[0] // groups)].astype(F32)
        out_ref[...] = (in_ref[...].astype(F32) * keep).astype(BF)

    return pl.pallas_call(
        kernel,
        grid_spec=pltpu.PrefetchScalarGridSpec(
            num_scalar_prefetch=1,
            grid=(steps,),
            in_specs=[pl.BlockSpec(block, lambda i, tab: (tab[0] * steps + i, 0, 0))],
            out_specs=pl.BlockSpec(block, lambda i, tab: (i, 0, 0)),
        ),
        out_shape=jax.ShapeDtypeStruct((rows,) + value.shape[1:], BF),
        compiler_params=pltpu.CompilerParams(vmem_limit_bytes=VMEM),
        cost_estimate=pl.CostEstimate(flops=1000, bytes_accessed=1000, transcendentals=0),
        name="masked_rows",
    )(table, value)


def g_kernel(tab_ref, own_ref, oth_ref, out_ref):
    tile = tab_ref[pl.program_id(0)]
    mine = tile // 2 == tab_ref[3]
    g = jnp.where(mine, own_ref[...].astype(F32), oth_ref[...].astype(F32)).astype(BF)
    n = g.shape[0]
    out_ref[...] = jnp.zeros_like(out_ref)
    out_ref[0, :n, :n] = g
    out_ref[0, n:, n:] = g


def g_pairs(own, other, table, width):
    def spec():
        return pl.BlockSpec((width, width), lambda i, tab: (tab[i] % 2, tab[2]))

    return pl.pallas_call(
        g_kernel,
        grid_spec=pltpu.PrefetchScalarGridSpec(
            num_scalar_prefetch=1,
            grid=(2,),
            in_specs=[spec(), spec()],
            out_specs=pl.BlockSpec((1, 2 * width, 2 * width), lambda i, tab: (i, 0, 0)),
        ),
        out_shape=jax.ShapeDtypeStruct((2, 2 * width, 2 * width), BF),
        compiler_params=pltpu.CompilerParams(vmem_limit_bytes=VMEM),
        cost_estimate=pl.CostEstimate(flops=1000, bytes_accessed=1000, transcendentals=0),
        name="g_pairs",
    )(table, own, other)


def body(
    coulomb_band, band_mask, dielectric, three_centre, centre_mask, greens, tile_map, batch_order
):
    rows = coulomb_band.shape[0]
    mus = three_centre.shape[1]
    width = three_centre.shape[2]
    z, x, c = lax.axis_index("z"), lax.axis_index("x"), lax.axis_index("core")
    s, h = lax.axis_index("sec"), lax.axis_index("ao")
    ri = (z * NX + x) * NC + c
    tiles = tile_map[:, 0]
    keep = jnp.repeat(centre_mask, rows // centre_mask.shape[0]).astype(BF)

    owners = batch_order[:, :4]
    own_owners = jnp.sum(jnp.where((jnp.arange(2) == s)[:, None], owners, 0), axis=0)
    wanted = jnp.concatenate([jnp.stack([ri, ri + 1 - 2 * c]).astype(jnp.int32), own_owners])
    all_places = jnp.arange(tiles.shape[0], dtype=jnp.int32)
    found = jnp.sum(jnp.where(wanted[:, None] == all_places[None, :], tiles[None, :], 0), axis=1)
    mine = jnp.arange(4, dtype=jnp.int32) == 2 * h + c
    my_tile = jnp.sum(jnp.where(mine, found[2:], 0)).reshape(1)
    ds, dh = jnp.array([0, 0, 1, 1] * 2), jnp.array([0, 1, 0, 1] * 2)
    to_core = jnp.array([1] * 4 + [0] * 4)
    flow = (s ^ ds) * 4 + (h ^ dh) * 2 + (c ^ to_core)
    flow_owner = jnp.sum(
        jnp.where(flow[:, None] == jnp.arange(8)[None, :], owners.reshape(1, -1), 0), axis=1
    ).astype(jnp.int32)
    table = flow_owner // NC
    here_now = (flow_owner[4:] % NC == c)[:, None, None, None]

    own_x = dielectric[0]
    ring = [(i, (i + 1) % (CHIPS * NC)) for i in range(CHIPS * NC)]
    back = [(j, i) for i, j in ring]
    before = lax.ppermute(own_x, ("z", "x", "core"), ring)
    behind = lax.ppermute(own_x, ("z", "x", "core"), back)
    g_other = shift(greens[0], "ao", 1)
    mask_full = jnp.repeat(jnp.repeat(band_mask, 64, axis=0), 64, axis=1).astype(BF)
    band = coulomb_band * mask_full
    stacked = jnp.concatenate([before, own_x, behind], axis=0)
    wt = lax.dot_general(stacked, band, (((0,), (1,)), ((), ())), preferred_element_type=F32).astype(BF)
    wt = wt * keep[None, :]
    wt = wt.reshape(2, rows, rows)
    half_rows = rows // 2
    q = half_rows // CHIPS
    wt_own = jnp.where(c == 0, wt[0], wt[1])
    wt_oth = shift(jnp.where(c == 0, wt[1], wt[0]), "core", 1)
    g2 = g_pairs(
        greens[0], g_other, jnp.concatenate([found[:2], my_tile, h.reshape(1)]).astype(jnp.int32), width
    )

    m_core = shift(three_centre, "core", 1)
    m_both = lax.ppermute(after(m_core, g_other), ("sec", "core", "ao"), along_y())

    send = after(masked_rows(three_centre, h, centre_mask), before, behind)
    spread = lax.all_to_all(send, ("z", "x"), 0, 0, tiled=True).reshape(CHIPS, q, mus, width)
    picked = pick(spread, table, 8, (m_both,))
    m_both = after(m_both, picked)
    m_sec = shift(m_both, "core", 1)
    ys_0 = y_part(None, 0, after(wt_own, picked), g2, three_centre)
    given = shift(picked[:4], "core", 1)
    pieces = jnp.where(here_now, picked[4:], given)
    got = [
        pieces[0],
        shift(pieces[1], "ao", 1),
        shift(pieces[2], "sec", 1),
        lax.ppermute(pieces[3], ("sec", "ao"), [(i, 3 - i) for i in range(4)]),
    ]
    got = jnp.stack(got).reshape(2, 2, q, mus, width)
    got = jnp.where(s == 0, got, got[::-1])
    got = jnp.where(h == 0, got, got[:, ::-1])
    halves = jnp.transpose(got, (1, 2, 0, 3, 4)).reshape(2, q, 2 * mus, width)
    piece_a, piece_b = halves[0], after(halves[1], ys_0)
    ys_1 = y_part(ys_0, 1, wt_oth, g2, m_core)
    ys_2 = y_part(ys_1, 3, wt_oth, g2, m_both)
    ys = y_part(ys_2, 2, wt_own, g2, m_sec)

    rel_z = [0]
    for step in range(1, NZ // 2):
        rel_z += [step, -step]
    rel_z.append(NZ // 2)
    lists = [], [], []

    def ids(first, zs, xs):
        start = len(lists[0])
        for dz in zs:
            for dx in xs:
                for entry, item in zip(lists, (first, dz, dx)):
                    entry.append(item)
        return start

    def ids_a(offset, first, count):
        return ids(0, [offset], list(range(first, first + count)))

    def ids_b(offset, first, count):
        return ids(CHIPS, rel_z[first : first + count], [offset])

    a_ids = {off: ids_a(off, 0, NX) for off in rel_z[:-1]}
    a_ids[4, 0], a_ids[4, 2] = ids_a(4, 0, 2), ids_a(4, 2, 2)
    b_ids = {off: ids_b(off, 0, NZ) for off in (0, 1, -1)}
    b_ids[2, 0], b_ids[2, 4] = ids_b(2, 0, 4), ids_b(2, 4, 4)
    first, off_z, off_x = (jnp.array(entry, jnp.int32) for entry in lists)
    places = first + ((z - off_z) % NZ) * NX + (x - off_x) % NX

    up, down = shift(piece_b, "z", 1), shift(piece_b, "z", -1)
    up, down = after(up, ys_1), after(down, ys_1)
    pieces = [piece_b, up, down]
    piece_a = after(piece_a, up, down)
    chunk_a = jnp.concatenate([piece_a] + [shift(piece_a, "x", d) for d in range(1, NX)], axis=0)
    up, down = shift(up, "z", 1), shift(down, "z", -1)
    up, down = after(up, ys_2), after(down, ys_2)
    pieces += [up, down]
    up, down = shift(up, "z", 1), shift(down, "z", -1)
    pieces += [up, down]
    pieces.append(shift(up, "z", 1))
    chunk_b = jnp.concatenate(pieces, axis=0)
    chunk_a = after(chunk_a, chunk_b)

    up1, down1 = shift(chunk_a, "z", 1), shift(chunk_a, "z", -1)
    up1, down1 = after(up1, ys), after(down1, ys)
    up_b, down_b = shift(chunk_b, "x", 1), shift(chunk_b, "x", -1)
    up2, down2 = shift(up1, "z", 1), shift(down1, "z", -1)
    total = contract(None, ys, places, [(chunk_a, a_ids[0]), (chunk_b, b_ids[0])], q)
    up2, down2 = after(up2, total), after(down2, total)
    up3, down3 = shift(up2, "z", 1), shift(down2, "z", -1)
    total = contract(total, ys, places, [(up1, a_ids[1]), (down1, a_ids[-1]), (up2, a_ids[2]), (down2, a_ids[-2])], q)
    up3, down3 = after(up3, total), after(down3, total)
    part = chunk_a.shape[0] // 2
    last_up, last_down = shift(up3[:part], "z", 1), shift(down3[part:], "z", -1)
    part_b = chunk_b.shape[0] // 2
    last_up_b, last_down_b = shift(up_b[:part_b], "x", 1), shift(down_b[part_b:], "x", -1)
    total = contract(total, ys, places, [(up3, a_ids[3]), (down3, a_ids[-3]), (up_b, b_ids[1]), (down_b, b_ids[-1])], q)
    total = contract(
        total,
        ys,
        places,
        [(last_up, a_ids[4, 0]), (last_down, a_ids[4, 2]), (last_up_b, b_ids[2, 0]), (last_down_b, b_ids[2, 4])],
        q,
    )

    total = -total
    row_places = jnp.arange(8, dtype=jnp.int32)
    starts = 2 * jnp.concatenate([found[:2], found[:2]]) + jnp.stack([s, s, 1 - s, 1 - s])
    here = starts[:, None] == row_places[None, :]
    partial = jnp.sum(jnp.where(here[:, :, None, None], total.reshape(4, 1, mus, width), 0.0), axis=0)
    partial = partial.reshape(8 * mus, width)
    moved = lax.all_to_all(partial, ("z", "x", "core", "ao"), 0, 0, tiled=True)
    own_rows = partial.shape[0] // (CHIPS * NC * 2)
    summed = jnp.sum(moved.reshape(CHIPS, NC, 2, own_rows, width), axis=0)
    col_places = jnp.arange(4, dtype=jnp.int32)
    there = found[2:].reshape(2, NC).T[:, :, None] == col_places
    out = jnp.sum(jnp.where(there[:, :, None, :, None], summed[:, :, :, None, :], 0.0), axis=(0, 1))
    return out.reshape(1, own_rows, 4 * width)


def solution(mesh):
    devices = mesh.devices.reshape(2, NZ, NX, NC, 2)
    split = Mesh(devices, ("sec", "z", "x", "core", "ao"))
    ri = ("z", "x", "core")
    placed = (
        P(ri, None),
        P(ri, None),
        P("sec", ri, "ao"),
        P(ri, "sec", None),
        P(ri),
        P("sec", "ao", None),
        P(),
        P(),
    )
    return jax.shard_map(
        body, mesh=split, in_specs=placed, out_specs=P("sec", ri + ("ao",), None), check_vma=False
    )
```

```python
import jax
import jax.numpy as jnp
from jax import lax
from jax.experimental import pallas as pl
from jax.experimental.pallas import tpu as pltpu
from jax.sharding import Mesh, PartitionSpec as P

NZ, NX, NC = 8, 4, 2
CHIPS = NZ * NX
VMEM = 60 << 20
BF = jnp.bfloat16
F32 = jnp.float32


def shift(value, axis, by):
    n = lax.axis_size(axis)
    return lax.ppermute(value, axis, [(i, (i + by) % n) for i in range(n)])


def along_y():
    pairs = []
    for y in range(4):
        for core, to in ((0, (y + 1) % 4), (1, (y + 3) % 4)):
            pairs.append(tuple(((p % 2) * NC + core) * 2 + p // 2 for p in (y, to)))
    return pairs


def y_kernel(wt_ref, g_ref, m_ref, y_ref):
    lane = m_ref.shape[2]
    m = jnp.swapaxes(m_ref[...], 0, 1)
    wt = wt_ref[...]
    g = g_ref[0]
    ys = []
    for mu in range(0, m.shape[0], 2):
        s = jnp.dot(wt, jnp.concatenate([m[mu], m[mu + 1]], axis=1), preferred_element_type=F32).astype(BF)
        y = jnp.dot(s, g, preferred_element_type=F32).astype(BF)
        ys += [y[:, :lane], y[:, lane:]]
    y_ref[...] = jnp.swapaxes(jnp.stack(ys), 0, 1)


def y_part(before, part, wt, g2, block):
    rows, mus, lane = block.shape
    group = 16
    steps = mus // group
    specs = [
        pl.BlockSpec((rows, rows), lambda i: (0, 0)),
        pl.BlockSpec((1, 2 * lane, 2 * lane), lambda i: (part % 2, 0, 0)),
        pl.BlockSpec((rows, group, lane), lambda i: (0, i, 0)),
    ]
    args = [wt, g2, block]
    aliases = {}
    kernel = y_kernel
    if before is not None:
        specs.append(pl.BlockSpec(memory_space=pl.ANY))
        args.append(before)
        aliases = {3: 0}

        def kernel(w, g, m, unused, *rest):
            y_kernel(w, g, m, *rest)

    return pl.pallas_call(
        kernel,
        grid=(steps,),
        in_specs=specs,
        out_specs=pl.BlockSpec((rows, group, lane), lambda i: (0, part * steps + i, 0)),
        out_shape=jax.ShapeDtypeStruct((rows, 4 * mus, lane), BF),
        input_output_aliases=aliases,
        compiler_params=pltpu.CompilerParams(vmem_limit_bytes=VMEM),
        cost_estimate=pl.CostEstimate(flops=40 * rows * rows * mus * lane, bytes_accessed=80 * rows * mus * lane, transcendentals=0),
        name="y_part",
    )(*args)


def after(value, *others, weight=0):
    return pl.pallas_call(
        lambda *refs: None,
        in_specs=[pl.BlockSpec(memory_space=pl.ANY)] * (1 + len(others)),
        out_specs=pl.BlockSpec(memory_space=pl.ANY),
        out_shape=jax.ShapeDtypeStruct(value.shape, value.dtype),
        input_output_aliases={0: 0},
        compiler_params=pltpu.CompilerParams(vmem_limit_bytes=VMEM),
        cost_estimate=pl.CostEstimate(
            flops=weight * 1000000000, bytes_accessed=weight * 3000000, transcendentals=0
        ),
        name="after",
    )(value, *others)


def contract_kernel(counts, more, tab_ref, *refs):
    out_ref = refs[-1]
    pieces = sum(counts)
    q = refs[0].shape[0]

    @pl.when(pl.program_id(0) == 0)
    def _():
        out_ref[...] = refs[-2][...] if more else jnp.zeros_like(out_ref)

    acc = out_ref[...]
    place = 0
    for source, count in enumerate(counts):
        f_ref = refs[pieces + source]
        for piece in range(count):
            y_ref = refs[place]
            place += 1
            for i in range(0, q, 2):
                lhs = jnp.concatenate([y_ref[i], y_ref[i + 1]], axis=1)
                rhs = jnp.concatenate([f_ref[piece * q + i], f_ref[piece * q + i + 1]], axis=1)
                acc += lax.dot_general(lhs, rhs, (((1,), (1,)), ((), ())), preferred_element_type=F32)
    out_ref[...] = acc


def contract(before, ys, table, chunks, q, steps=2):
    values = [value for value, _ in chunks]
    counts = [value.shape[0] // q // steps for value in values]
    per = sum(counts)
    rows, lane = ys.shape[1], ys.shape[2]
    nus = values[0].shape[1]

    def y_spec(start, count):
        return pl.BlockSpec((q, rows, lane), lambda i, tab: (tab[start + i * count], 0, 0))

    specs = [
        y_spec(start + piece, count)
        for (_, start), count in zip(chunks, counts)
        for piece in range(count)
    ]
    specs += [pl.BlockSpec((count * q, nus, lane), lambda i, tab: (i, 0, 0)) for count in counts]
    args = [table] + [ys] * per + values
    if before is not None:
        specs.append(pl.BlockSpec((rows, nus), lambda i, tab: (0, 0)))
        args.append(before)
    return pl.pallas_call(
        lambda *refs: contract_kernel(counts, before is not None, *refs),
        grid_spec=pltpu.PrefetchScalarGridSpec(
            num_scalar_prefetch=1,
            grid=(steps,),
            in_specs=specs,
            out_specs=pl.BlockSpec((rows, nus), lambda i, tab: (0, 0)),
        ),
        out_shape=jax.ShapeDtypeStruct((rows, nus), F32),
        compiler_params=pltpu.CompilerParams(vmem_limit_bytes=VMEM),
        cost_estimate=pl.CostEstimate(
            flops=2 * rows * nus * lane * q * per * steps,
            bytes_accessed=2 * q * per * steps * lane * (rows + nus),
            transcendentals=0,
        ),
        name="contract",
    )(*args)


def pick(buffer, table, count, others):
    block = (1,) + buffer.shape[1:]
    zeros = (0,) * (buffer.ndim - 1)

    def spec(i):
        return pl.BlockSpec(block, lambda j, tab: (tab[i],) + zeros)

    def kernel(tab_ref, *refs):
        for i in range(count):
            refs[-1][i] = refs[i][0]

    return pl.pallas_call(
        kernel,
        grid_spec=pltpu.PrefetchScalarGridSpec(
            num_scalar_prefetch=1,
            grid=(1,),
            in_specs=[spec(i) for i in range(count)] + [pl.BlockSpec(memory_space=pl.ANY)] * len(others),
            out_specs=pl.BlockSpec((count,) + buffer.shape[1:], lambda j, tab: (0,) + zeros),
        ),
        out_shape=jax.ShapeDtypeStruct((count,) + buffer.shape[1:], buffer.dtype),
        compiler_params=pltpu.CompilerParams(vmem_limit_bytes=VMEM),
        cost_estimate=pl.CostEstimate(flops=1000, bytes_accessed=1000, transcendentals=0),
        name="pick",
    )(table, *([buffer] * count), *others)


def masked_rows(value, half, mask):
    groups = mask.shape[0]
    steps = 2
    rows = value.shape[0] // 2
    step_rows = rows // steps
    table = jnp.concatenate([half.reshape(1), mask]).astype(jnp.int32)
    block = (step_rows,) + value.shape[1:]

    def kernel(tab_ref, in_ref, out_ref):
        row = tab_ref[0] * rows + pl.program_id(0) * step_rows
        keep = tab_ref[1 + row // (value.shape[0] // groups)].astype(F32)
        out_ref[...] = (in_ref[...].astype(F32) * keep).astype(BF)

    return pl.pallas_call(
        kernel,
        grid_spec=pltpu.PrefetchScalarGridSpec(
            num_scalar_prefetch=1,
            grid=(steps,),
            in_specs=[pl.BlockSpec(block, lambda i, tab: (tab[0] * steps + i, 0, 0))],
            out_specs=pl.BlockSpec(block, lambda i, tab: (i, 0, 0)),
        ),
        out_shape=jax.ShapeDtypeStruct((rows,) + value.shape[1:], BF),
        compiler_params=pltpu.CompilerParams(vmem_limit_bytes=VMEM),
        cost_estimate=pl.CostEstimate(flops=1000, bytes_accessed=1000, transcendentals=0),
        name="masked_rows",
    )(table, value)


def g_kernel(tab_ref, own_ref, oth_ref, out_ref):
    tile = tab_ref[pl.program_id(0)]
    mine = tile // 2 == tab_ref[3]
    g = jnp.where(mine, own_ref[...].astype(F32), oth_ref[...].astype(F32)).astype(BF)
    n = g.shape[0]
    out_ref[...] = jnp.zeros_like(out_ref)
    out_ref[0, :n, :n] = g
    out_ref[0, n:, n:] = g


def g_pairs(own, other, table, width):
    def spec():
        return pl.BlockSpec((width, width), lambda i, tab: (tab[i] % 2, tab[2]))

    return pl.pallas_call(
        g_kernel,
        grid_spec=pltpu.PrefetchScalarGridSpec(
            num_scalar_prefetch=1,
            grid=(2,),
            in_specs=[spec(), spec()],
            out_specs=pl.BlockSpec((1, 2 * width, 2 * width), lambda i, tab: (i, 0, 0)),
        ),
        out_shape=jax.ShapeDtypeStruct((2, 2 * width, 2 * width), BF),
        compiler_params=pltpu.CompilerParams(vmem_limit_bytes=VMEM),
        cost_estimate=pl.CostEstimate(flops=1000, bytes_accessed=1000, transcendentals=0),
        name="g_pairs",
    )(table, own, other)


def body(
    coulomb_band, band_mask, dielectric, three_centre, centre_mask, greens, tile_map, batch_order
):
    rows = coulomb_band.shape[0]
    mus = three_centre.shape[1]
    width = three_centre.shape[2]
    z, x, c = lax.axis_index("z"), lax.axis_index("x"), lax.axis_index("core")
    s, h = lax.axis_index("sec"), lax.axis_index("ao")
    ri = (z * NX + x) * NC + c
    tiles = tile_map[:, 0]
    keep = jnp.repeat(centre_mask, rows // centre_mask.shape[0]).astype(BF)

    owners = batch_order[:, :4]
    own_owners = jnp.sum(jnp.where((jnp.arange(2) == s)[:, None], owners, 0), axis=0)
    wanted = jnp.concatenate([jnp.stack([ri, ri + 1 - 2 * c]).astype(jnp.int32), own_owners])
    all_places = jnp.arange(tiles.shape[0], dtype=jnp.int32)
    found = jnp.sum(jnp.where(wanted[:, None] == all_places[None, :], tiles[None, :], 0), axis=1)
    mine = jnp.arange(4, dtype=jnp.int32) == 2 * h + c
    my_tile = jnp.sum(jnp.where(mine, found[2:], 0)).reshape(1)
    ds, dh = jnp.array([0, 0, 1, 1] * 2), jnp.array([0, 1, 0, 1] * 2)
    to_core = jnp.array([1] * 4 + [0] * 4)
    flow = (s ^ ds) * 4 + (h ^ dh) * 2 + (c ^ to_core)
    flow_owner = jnp.sum(
        jnp.where(flow[:, None] == jnp.arange(8)[None, :], owners.reshape(1, -1), 0), axis=1
    ).astype(jnp.int32)
    table = flow_owner // NC
    here_now = (flow_owner[4:] % NC == c)[:, None, None, None]

    own_x = dielectric[0]
    ring = [(i, (i + 1) % (CHIPS * NC)) for i in range(CHIPS * NC)]
    back = [(j, i) for i, j in ring]
    before = lax.ppermute(own_x, ("z", "x", "core"), ring)
    behind = lax.ppermute(own_x, ("z", "x", "core"), back)
    g_other = shift(greens[0], "ao", 1)
    mask_full = jnp.repeat(jnp.repeat(band_mask, 64, axis=0), 64, axis=1).astype(BF)
    band = coulomb_band * mask_full
    stacked = jnp.concatenate([before, own_x, behind], axis=0)
    wt = lax.dot_general(stacked, band, (((0,), (1,)), ((), ())), preferred_element_type=F32).astype(BF)
    wt = wt * keep[None, :]
    wt = wt.reshape(2, rows, rows)
    half_rows = rows // 2
    q = half_rows // CHIPS
    wt_own = jnp.where(c == 0, wt[0], wt[1])
    wt_oth = shift(jnp.where(c == 0, wt[1], wt[0]), "core", 1)
    g2 = g_pairs(
        greens[0], g_other, jnp.concatenate([found[:2], my_tile, h.reshape(1)]).astype(jnp.int32), width
    )

    m_core = after(shift(three_centre, "core", 1), g_other)
    m_both = lax.ppermute(m_core, ("sec", "core", "ao"), along_y())

    send = after(masked_rows(three_centre, h, centre_mask), before, behind)
    spread = lax.all_to_all(send, ("z", "x"), 0, 0, tiled=True).reshape(CHIPS, q, mus, width)
    picked = pick(spread, table, 8, (m_both,))
    m_both = after(m_both, picked)
    m_sec = shift(m_both, "core", 1)
    ys_0 = y_part(None, 0, after(wt_own, picked), g2, three_centre)
    given = shift(picked[:4], "core", 1)
    pieces = jnp.where(here_now, picked[4:], given)
    got = [
        pieces[0],
        shift(pieces[1], "ao", 1),
        shift(pieces[2], "sec", 1),
        lax.ppermute(pieces[3], ("sec", "ao"), [(i, 3 - i) for i in range(4)]),
    ]
    got = jnp.stack(got).reshape(2, 2, q, mus, width)
    got = jnp.where(s == 0, got, got[::-1])
    got = jnp.where(h == 0, got, got[:, ::-1])
    halves = jnp.transpose(got, (1, 2, 0, 3, 4)).reshape(2, q, 2 * mus, width)
    piece_a, piece_b = halves[0], after(halves[1], ys_0)
    ys_1 = y_part(ys_0, 1, wt_oth, g2, m_core)
    ys_2 = y_part(ys_1, 3, wt_oth, g2, m_both)
    ys = y_part(ys_2, 2, wt_own, g2, m_sec)

    rel_z = [0]
    for step in range(1, NZ // 2):
        rel_z += [step, -step]
    rel_z.append(NZ // 2)
    lists = [], [], []

    def ids(first, zs, xs):
        start = len(lists[0])
        for dz in zs:
            for dx in xs:
                for entry, item in zip(lists, (first, dz, dx)):
                    entry.append(item)
        return start

    def ids_a(offset, first, count):
        return ids(0, [offset], list(range(first, first + count)))

    def ids_b(offset, first, count):
        return ids(CHIPS, rel_z[first : first + count], [offset])

    a_ids = {off: ids_a(off, 0, NX) for off in rel_z[:-1]}
    a_ids[4, 0], a_ids[4, 2] = ids_a(4, 0, 2), ids_a(4, 2, 2)
    b_ids = {off: ids_b(off, 0, NZ) for off in (0, 1, -1)}
    b_ids[2, 0], b_ids[2, 4] = ids_b(2, 0, 4), ids_b(2, 4, 4)
    first, off_z, off_x = (jnp.array(entry, jnp.int32) for entry in lists)
    places = first + ((z - off_z) % NZ) * NX + (x - off_x) % NX

    up, down = shift(piece_b, "z", 1), shift(piece_b, "z", -1)
    up, down = after(up, ys_1), after(down, ys_1)
    pieces = [piece_b, up, down]
    piece_a = after(piece_a, up, down)
    chunk_a = jnp.concatenate([piece_a] + [shift(piece_a, "x", d) for d in range(1, NX)], axis=0)
    up, down = shift(up, "z", 1), shift(down, "z", -1)
    up, down = after(up, ys_2), after(down, ys_2)
    pieces += [up, down]
    up, down = shift(up, "z", 1), shift(down, "z", -1)
    pieces += [up, down]
    pieces.append(shift(up, "z", 1))
    chunk_b = jnp.concatenate(pieces, axis=0)
    chunk_a = after(chunk_a, chunk_b)

    up1, down1 = shift(chunk_a, "z", 1), shift(chunk_a, "z", -1)
    up1, down1 = after(up1, ys), after(down1, ys)
    up_b, down_b = shift(chunk_b, "x", 1), shift(chunk_b, "x", -1)
    up2, down2 = shift(up1, "z", 1), shift(down1, "z", -1)
    total = contract(None, ys, places, [(chunk_a, a_ids[0]), (chunk_b, b_ids[0])], q)
    up2, down2 = after(up2, total), after(down2, total)
    up3, down3 = shift(up2, "z", 1), shift(down2, "z", -1)
    total = contract(total, ys, places, [(up1, a_ids[1]), (down1, a_ids[-1]), (up2, a_ids[2]), (down2, a_ids[-2])], q)
    up3, down3 = after(up3, total), after(down3, total)
    part = chunk_a.shape[0] // 2
    last_up, last_down = shift(up3[:part], "z", 1), shift(down3[part:], "z", -1)
    part_b = chunk_b.shape[0] // 2
    last_up_b, last_down_b = shift(up_b[:part_b], "x", 1), shift(down_b[part_b:], "x", -1)
    total = contract(
        total,
        ys,
        places,
        [
            (up3, a_ids[3]),
            (down3, a_ids[-3]),
            (up_b, b_ids[1]),
            (down_b, b_ids[-1]),
            (last_up_b, b_ids[2, 0]),
            (last_down_b, b_ids[2, 4]),
        ],
        q,
    )
    total = contract(total, ys, places, [(last_up, a_ids[4, 0]), (last_down, a_ids[4, 2])], q)

    row_places = jnp.arange(8, dtype=jnp.int32)
    starts = 2 * jnp.concatenate([found[:2], found[:2]]) + jnp.stack([s, s, 1 - s, 1 - s])
    here = starts[:, None] == row_places[None, :]
    partial = jnp.sum(jnp.where(here[:, :, None, None], total.reshape(4, 1, mus, width), 0.0), axis=0)
    partial = partial.reshape(8 * mus, width)
    moved = lax.all_to_all(partial, ("z", "x", "core", "ao"), 0, 0, tiled=True)
    own_rows = partial.shape[0] // (CHIPS * NC * 2)
    summed = jnp.sum(moved.reshape(CHIPS, NC, 2, own_rows, width), axis=0)
    col_places = jnp.arange(4, dtype=jnp.int32)
    there = found[2:].reshape(2, NC).T[:, :, None] == col_places
    out = -jnp.sum(jnp.where(there[:, :, None, :, None], summed[:, :, :, None, :], 0.0), axis=(0, 1))
    return out.reshape(1, own_rows, 4 * width)


def solution(mesh):
    devices = mesh.devices.reshape(2, NZ, NX, NC, 2)
    split = Mesh(devices, ("sec", "z", "x", "core", "ao"))
    ri = ("z", "x", "core")
    placed = (
        P(ri, None),
        P(ri, None),
        P("sec", ri, "ao"),
        P(ri, "sec", None),
        P(ri),
        P("sec", "ao", None),
        P(),
        P(),
    )
    return jax.shard_map(
        body, mesh=split, in_specs=placed, out_specs=P("sec", ri + ("ao",), None), check_vma=False
    )
```

```python
import jax
import jax.numpy as jnp
from jax import lax
from jax.experimental import pallas as pl
from jax.experimental.pallas import tpu as pltpu
from jax.sharding import Mesh, PartitionSpec as P

NZ, NX, NC = 8, 4, 2
CHIPS = NZ * NX
VMEM = 52 << 20
BF = jnp.bfloat16
F32 = jnp.float32


def shift(value, axis, by):
    n = lax.axis_size(axis)
    return lax.ppermute(value, axis, [(i, (i + by) % n) for i in range(n)])


def along_y():
    pairs = []
    for y in range(4):
        for core, to in ((0, (y + 1) % 4), (1, (y + 3) % 4)):
            pairs.append(tuple(((p % 2) * NC + core) * 2 + p // 2 for p in (y, to)))
    return pairs


def y_kernel(wt_ref, g_ref, m_ref, y_ref):
    lane = m_ref.shape[2]
    m = jnp.swapaxes(m_ref[...], 0, 1)
    wt = wt_ref[...]
    g = g_ref[0]
    ys = []
    for mu in range(0, m.shape[0], 2):
        s = jnp.dot(wt, jnp.concatenate([m[mu], m[mu + 1]], axis=1), preferred_element_type=F32).astype(BF)
        y = jnp.dot(s, g, preferred_element_type=F32).astype(BF)
        ys += [y[:, :lane], y[:, lane:]]
    y_ref[...] = jnp.swapaxes(jnp.stack(ys), 0, 1)


def y_part(before, part, wt, g2, block):
    rows, mus, lane = block.shape
    group = 16
    steps = mus // group
    specs = [
        pl.BlockSpec((rows, rows), lambda i: (0, 0)),
        pl.BlockSpec((1, 2 * lane, 2 * lane), lambda i: (part % 2, 0, 0)),
        pl.BlockSpec((rows, group, lane), lambda i: (0, i, 0)),
    ]
    args = [wt, g2, block]
    aliases = {}
    kernel = y_kernel
    if before is not None:
        specs.append(pl.BlockSpec(memory_space=pl.ANY))
        args.append(before)
        aliases = {3: 0}

        def kernel(w, g, m, unused, *rest):
            y_kernel(w, g, m, *rest)

    return pl.pallas_call(
        kernel,
        grid=(steps,),
        in_specs=specs,
        out_specs=pl.BlockSpec((rows, group, lane), lambda i: (0, part * steps + i, 0)),
        out_shape=jax.ShapeDtypeStruct((rows, 4 * mus, lane), BF),
        input_output_aliases=aliases,
        compiler_params=pltpu.CompilerParams(vmem_limit_bytes=VMEM),
        cost_estimate=pl.CostEstimate(flops=40 * rows * rows * mus * lane, bytes_accessed=80 * rows * mus * lane, transcendentals=0),
        name="y_part",
    )(*args)


def after(value, *others, weight=0):
    return pl.pallas_call(
        lambda *refs: None,
        in_specs=[pl.BlockSpec(memory_space=pl.ANY)] * (1 + len(others)),
        out_specs=pl.BlockSpec(memory_space=pl.ANY),
        out_shape=jax.ShapeDtypeStruct(value.shape, value.dtype),
        input_output_aliases={0: 0},
        compiler_params=pltpu.CompilerParams(vmem_limit_bytes=VMEM),
        cost_estimate=pl.CostEstimate(
            flops=weight * 1000000000, bytes_accessed=weight * 3000000, transcendentals=0
        ),
        name="after",
    )(value, *others)


def contract_kernel(counts, more, tab_ref, *refs):
    out_ref = refs[-1]
    pieces = sum(counts)
    q = refs[0].shape[0]

    @pl.when(pl.program_id(0) == 0)
    def _():
        out_ref[...] = refs[-2][...] if more else jnp.zeros_like(out_ref)

    acc = out_ref[...]
    place = 0
    for source, count in enumerate(counts):
        f_ref = refs[pieces + source]
        for piece in range(count):
            y_ref = refs[place]
            place += 1
            for i in range(0, q, 2):
                lhs = jnp.concatenate([y_ref[i], y_ref[i + 1]], axis=1)
                rhs = jnp.concatenate([f_ref[piece * q + i], f_ref[piece * q + i + 1]], axis=1)
                acc += lax.dot_general(lhs, rhs, (((1,), (1,)), ((), ())), preferred_element_type=F32)
    out_ref[...] = acc


def contract(before, ys, table, chunks, q, steps=2):
    values = [value for value, _ in chunks]
    counts = [value.shape[0] // q // steps for value in values]
    per = sum(counts)
    rows, lane = ys.shape[1], ys.shape[2]
    nus = values[0].shape[1]

    def y_spec(start, count):
        return pl.BlockSpec((q, rows, lane), lambda i, tab: (tab[start + i * count], 0, 0))

    specs = [
        y_spec(start + piece, count)
        for (_, start), count in zip(chunks, counts)
        for piece in range(count)
    ]
    specs += [pl.BlockSpec((count * q, nus, lane), lambda i, tab: (i, 0, 0)) for count in counts]
    args = [table] + [ys] * per + values
    if before is not None:
        specs.append(pl.BlockSpec((rows, nus), lambda i, tab: (0, 0)))
        args.append(before)
    return pl.pallas_call(
        lambda *refs: contract_kernel(counts, before is not None, *refs),
        grid_spec=pltpu.PrefetchScalarGridSpec(
            num_scalar_prefetch=1,
            grid=(steps,),
            in_specs=specs,
            out_specs=pl.BlockSpec((rows, nus), lambda i, tab: (0, 0)),
        ),
        out_shape=jax.ShapeDtypeStruct((rows, nus), F32),
        compiler_params=pltpu.CompilerParams(vmem_limit_bytes=VMEM),
        cost_estimate=pl.CostEstimate(
            flops=2 * rows * nus * lane * q * per * steps,
            bytes_accessed=2 * q * per * steps * lane * (rows + nus),
            transcendentals=0,
        ),
        name="contract",
    )(*args)


def pick(buffer, table, count, others):
    block = (1,) + buffer.shape[1:]
    zeros = (0,) * (buffer.ndim - 1)

    def spec(i):
        return pl.BlockSpec(block, lambda j, tab: (tab[i],) + zeros)

    def kernel(tab_ref, *refs):
        for i in range(count):
            refs[-1][i] = refs[i][0]

    return pl.pallas_call(
        kernel,
        grid_spec=pltpu.PrefetchScalarGridSpec(
            num_scalar_prefetch=1,
            grid=(1,),
            in_specs=[spec(i) for i in range(count)] + [pl.BlockSpec(memory_space=pl.ANY)] * len(others),
            out_specs=pl.BlockSpec((count,) + buffer.shape[1:], lambda j, tab: (0,) + zeros),
        ),
        out_shape=jax.ShapeDtypeStruct((count,) + buffer.shape[1:], buffer.dtype),
        compiler_params=pltpu.CompilerParams(vmem_limit_bytes=VMEM),
        cost_estimate=pl.CostEstimate(flops=1000, bytes_accessed=1000, transcendentals=0),
        name="pick",
    )(table, *([buffer] * count), *others)


def masked_rows(value, half, mask):
    groups = mask.shape[0]
    steps = 2
    rows = value.shape[0] // 2
    step_rows = rows // steps
    table = jnp.concatenate([half.reshape(1), mask]).astype(jnp.int32)
    block = (step_rows,) + value.shape[1:]

    def kernel(tab_ref, in_ref, out_ref):
        row = tab_ref[0] * rows + pl.program_id(0) * step_rows
        keep = tab_ref[1 + row // (value.shape[0] // groups)].astype(F32)
        out_ref[...] = (in_ref[...].astype(F32) * keep).astype(BF)

    return pl.pallas_call(
        kernel,
        grid_spec=pltpu.PrefetchScalarGridSpec(
            num_scalar_prefetch=1,
            grid=(steps,),
            in_specs=[pl.BlockSpec(block, lambda i, tab: (tab[0] * steps + i, 0, 0))],
            out_specs=pl.BlockSpec(block, lambda i, tab: (i, 0, 0)),
        ),
        out_shape=jax.ShapeDtypeStruct((rows,) + value.shape[1:], BF),
        compiler_params=pltpu.CompilerParams(vmem_limit_bytes=VMEM),
        cost_estimate=pl.CostEstimate(flops=1000, bytes_accessed=1000, transcendentals=0),
        name="masked_rows",
    )(table, value)


def g_kernel(tab_ref, own_ref, oth_ref, out_ref):
    tile = tab_ref[pl.program_id(0)]
    mine = tile // 2 == tab_ref[3]
    g = jnp.where(mine, own_ref[...].astype(F32), oth_ref[...].astype(F32)).astype(BF)
    n = g.shape[0]
    out_ref[...] = jnp.zeros_like(out_ref)
    out_ref[0, :n, :n] = g
    out_ref[0, n:, n:] = g


def g_pairs(own, other, table, width):
    def spec():
        return pl.BlockSpec((width, width), lambda i, tab: (tab[i] % 2, tab[2]))

    return pl.pallas_call(
        g_kernel,
        grid_spec=pltpu.PrefetchScalarGridSpec(
            num_scalar_prefetch=1,
            grid=(2,),
            in_specs=[spec(), spec()],
            out_specs=pl.BlockSpec((1, 2 * width, 2 * width), lambda i, tab: (i, 0, 0)),
        ),
        out_shape=jax.ShapeDtypeStruct((2, 2 * width, 2 * width), BF),
        compiler_params=pltpu.CompilerParams(vmem_limit_bytes=VMEM),
        cost_estimate=pl.CostEstimate(flops=1000, bytes_accessed=1000, transcendentals=0),
        name="g_pairs",
    )(table, own, other)


def body(
    coulomb_band, band_mask, dielectric, three_centre, centre_mask, greens, tile_map, batch_order
):
    rows = coulomb_band.shape[0]
    mus = three_centre.shape[1]
    width = three_centre.shape[2]
    z, x, c = lax.axis_index("z"), lax.axis_index("x"), lax.axis_index("core")
    s, h = lax.axis_index("sec"), lax.axis_index("ao")
    ri = (z * NX + x) * NC + c
    tiles = tile_map[:, 0]
    keep = jnp.repeat(centre_mask, rows // centre_mask.shape[0]).astype(BF)

    owners = batch_order[:, :4]
    own_owners = jnp.sum(jnp.where((jnp.arange(2) == s)[:, None], owners, 0), axis=0)
    wanted = jnp.concatenate([jnp.stack([ri, ri + 1 - 2 * c]).astype(jnp.int32), own_owners])
    all_places = jnp.arange(tiles.shape[0], dtype=jnp.int32)
    found = jnp.sum(jnp.where(wanted[:, None] == all_places[None, :], tiles[None, :], 0), axis=1)
    mine = jnp.arange(4, dtype=jnp.int32) == 2 * h + c
    my_tile = jnp.sum(jnp.where(mine, found[2:], 0)).reshape(1)
    ds, dh = jnp.array([0, 0, 1, 1] * 2), jnp.array([0, 1, 0, 1] * 2)
    to_core = jnp.array([1] * 4 + [0] * 4)
    flow = (s ^ ds) * 4 + (h ^ dh) * 2 + (c ^ to_core)
    flow_owner = jnp.sum(
        jnp.where(flow[:, None] == jnp.arange(8)[None, :], owners.reshape(1, -1), 0), axis=1
    ).astype(jnp.int32)
    table = flow_owner // NC
    here_now = (flow_owner[4:] % NC == c)[:, None, None, None]

    send = masked_rows(three_centre, h, centre_mask)
    own_x = after(dielectric[0], send)
    ring = [(i, (i + 1) % (CHIPS * NC)) for i in range(CHIPS * NC)]
    back = [(j, i) for i, j in ring]
    before = lax.ppermute(own_x, ("z", "x", "core"), ring)
    behind = lax.ppermute(own_x, ("z", "x", "core"), back)
    g_other = shift(greens[0], "ao", 1)
    mask_full = jnp.repeat(jnp.repeat(band_mask, 64, axis=0), 64, axis=1).astype(BF)
    band = coulomb_band * mask_full
    stacked = jnp.concatenate([before, own_x, behind], axis=0)
    wt = lax.dot_general(stacked, band, (((0,), (1,)), ((), ())), preferred_element_type=F32).astype(BF)
    wt = wt * keep[None, :]
    wt = wt.reshape(2, rows, rows)
    half_rows = rows // 2
    q = half_rows // CHIPS
    wt_own = jnp.where(c == 0, wt[0], wt[1])
    wt_oth = shift(jnp.where(c == 0, wt[1], wt[0]), "core", 1)
    g2 = g_pairs(
        greens[0], g_other, jnp.concatenate([found[:2], my_tile, h.reshape(1)]).astype(jnp.int32), width
    )

    m_core = after(shift(three_centre, "core", 1), g_other)
    m_both = lax.ppermute(m_core, ("sec", "core", "ao"), along_y())

    send = after(send, before, behind)
    spread = lax.all_to_all(send, ("z", "x"), 0, 0, tiled=True).reshape(CHIPS, q, mus, width)
    picked = pick(spread, table, 8, (m_both,))
    m_both = after(m_both, picked)
    m_sec = shift(m_both, "core", 1)
    ys_0 = y_part(None, 0, after(wt_own, picked), g2, three_centre)
    given = shift(picked[:4], "core", 1)
    pieces = jnp.where(here_now, picked[4:], given)
    got = [
        pieces[0],
        shift(pieces[1], "ao", 1),
        shift(pieces[2], "sec", 1),
        lax.ppermute(pieces[3], ("sec", "ao"), [(i, 3 - i) for i in range(4)]),
    ]
    got = jnp.stack(got).reshape(2, 2, q, mus, width)
    got = jnp.where(s == 0, got, got[::-1])
    got = jnp.where(h == 0, got, got[:, ::-1])
    halves = jnp.transpose(got, (1, 2, 0, 3, 4)).reshape(2, q, 2 * mus, width)
    piece_a, piece_b = halves[0], after(halves[1], ys_0)
    ys_1 = y_part(ys_0, 1, wt_oth, g2, m_core)
    ys_2 = y_part(ys_1, 3, wt_oth, g2, m_both)
    ys = y_part(ys_2, 2, wt_own, g2, m_sec)

    rel_z = [0]
    for step in range(1, NZ // 2):
        rel_z += [step, -step]
    rel_z.append(NZ // 2)
    lists = [], [], []

    def ids(first, zs, xs):
        start = len(lists[0])
        for dz in zs:
            for dx in xs:
                for entry, item in zip(lists, (first, dz, dx)):
                    entry.append(item)
        return start

    def ids_a(offset, first, count):
        return ids(0, [offset], list(range(first, first + count)))

    def ids_b(offset, first, count):
        return ids(CHIPS, rel_z[first : first + count], [offset])

    a_ids = {off: ids_a(off, 0, NX) for off in rel_z[:-1]}
    a_ids[4, 0], a_ids[4, 2] = ids_a(4, 0, 2), ids_a(4, 2, 2)
    b_ids = {off: ids_b(off, 0, NZ) for off in (0, 1, -1)}
    b_ids[2, 0], b_ids[2, 4] = ids_b(2, 0, 4), ids_b(2, 4, 4)
    first, off_z, off_x = (jnp.array(entry, jnp.int32) for entry in lists)
    places = first + ((z - off_z) % NZ) * NX + (x - off_x) % NX

    up, down = shift(piece_b, "z", 1), shift(piece_b, "z", -1)
    up, down = after(up, ys_1), after(down, ys_1)
    pieces = [piece_b, up, down]
    piece_a = after(piece_a, up, down)
    chunk_a = jnp.concatenate([piece_a] + [shift(piece_a, "x", d) for d in range(1, NX)], axis=0)
    up, down = shift(up, "z", 1), shift(down, "z", -1)
    pieces += [up, down]
    up, down = shift(up, "z", 1), shift(down, "z", -1)
    pieces += [up, down]
    pieces.append(shift(up, "z", 1))
    chunk_b = jnp.concatenate(pieces, axis=0)
    chunk_a = after(chunk_a, chunk_b)

    up1, down1 = shift(chunk_a, "z", 1), shift(chunk_a, "z", -1)
    up1, down1 = after(up1, ys_2), after(down1, ys_2)
    up_b, down_b = shift(chunk_b, "x", 1), shift(chunk_b, "x", -1)
    up2, down2 = shift(up1, "z", 1), shift(down1, "z", -1)
    up2, down2 = after(up2, ys), after(down2, ys)
    up3, down3 = shift(up2, "z", 1), shift(down2, "z", -1)
    total = contract(
        None,
        ys,
        places,
        [
            (chunk_a, a_ids[0]),
            (chunk_b, b_ids[0]),
        ],
        q,
    )
    up3, down3 = after(up3, total), after(down3, total)
    part = chunk_a.shape[0] // 2
    last_up, last_down = shift(up3[:part], "z", 1), shift(down3[part:], "z", -1)
    part_b = chunk_b.shape[0] // 2
    last_up_b, last_down_b = shift(up_b[:part_b], "x", 1), shift(down_b[part_b:], "x", -1)
    total = contract(
        total,
        ys,
        places,
        [
            (up1, a_ids[1]),
            (down1, a_ids[-1]),
            (up2, a_ids[2]),
            (down2, a_ids[-2]),
            (up3, a_ids[3]),
            (down3, a_ids[-3]),
            (up_b, b_ids[1]),
            (down_b, b_ids[-1]),
            (last_up_b, b_ids[2, 0]),
            (last_down_b, b_ids[2, 4]),
        ],
        q,
    )
    total = contract(total, ys, places, [(last_up, a_ids[4, 0]), (last_down, a_ids[4, 2])], q)

    row_places = jnp.arange(8, dtype=jnp.int32)
    starts = 2 * jnp.concatenate([found[:2], found[:2]]) + jnp.stack([s, s, 1 - s, 1 - s])
    here = starts[:, None] == row_places[None, :]
    partial = jnp.sum(jnp.where(here[:, :, None, None], total.reshape(4, 1, mus, width), 0.0), axis=0)
    partial = partial.reshape(8 * mus, width)
    moved = lax.all_to_all(partial, ("z", "x", "core", "ao"), 0, 0, tiled=True)
    own_rows = partial.shape[0] // (CHIPS * NC * 2)
    summed = jnp.sum(moved.reshape(CHIPS, NC, 2, own_rows, width), axis=0)
    col_places = jnp.arange(4, dtype=jnp.int32)
    there = found[2:].reshape(2, NC).T[:, :, None] == col_places
    out = -jnp.sum(jnp.where(there[:, :, None, :, None], summed[:, :, :, None, :], 0.0), axis=(0, 1))
    return out.reshape(1, own_rows, 4 * width)


def solution(mesh):
    devices = mesh.devices.reshape(2, NZ, NX, NC, 2)
    split = Mesh(devices, ("sec", "z", "x", "core", "ao"))
    ri = ("z", "x", "core")
    placed = (
        P(ri, None),
        P(ri, None),
        P("sec", ri, "ao"),
        P(ri, "sec", None),
        P(ri),
        P("sec", "ao", None),
        P(),
        P(),
    )
    return jax.shard_map(
        body, mesh=split, in_specs=placed, out_specs=P("sec", ri + ("ao",), None), check_vma=False
    )
```

```python
import jax
import jax.numpy as jnp
from jax import lax
from jax.experimental import pallas as pl
from jax.experimental.pallas import tpu as pltpu
from jax.sharding import Mesh, PartitionSpec as P

NZ, NX, NC = 8, 4, 2
CHIPS = NZ * NX
VMEM = 49 << 20
BF = jnp.bfloat16
F32 = jnp.float32


def shift(value, axis, by):
    n = lax.axis_size(axis)
    return lax.ppermute(value, axis, [(i, (i + by) % n) for i in range(n)])


def along_y():
    pairs = []
    for y in range(4):
        for core, to in ((0, (y + 1) % 4), (1, (y + 3) % 4)):
            pairs.append(tuple(((p % 2) * NC + core) * 2 + p // 2 for p in (y, to)))
    return pairs


def y_kernel(wt_ref, g_ref, m_ref, y_ref):
    lane = m_ref.shape[2]
    m = jnp.swapaxes(m_ref[...], 0, 1)
    wt = wt_ref[...]
    g = g_ref[0]
    ys = []
    for mu in range(0, m.shape[0], 2):
        s = jnp.dot(wt, jnp.concatenate([m[mu], m[mu + 1]], axis=1), preferred_element_type=F32).astype(BF)
        y = jnp.dot(s, g, preferred_element_type=F32).astype(BF)
        ys += [y[:, :lane], y[:, lane:]]
    y_ref[...] = jnp.swapaxes(jnp.stack(ys), 0, 1)


def y_part(before, part, wt, g2, block):
    rows, mus, lane = block.shape
    group = 16
    steps = mus // group
    specs = [
        pl.BlockSpec((rows, rows), lambda i: (0, 0)),
        pl.BlockSpec((1, 2 * lane, 2 * lane), lambda i: (part % 2, 0, 0)),
        pl.BlockSpec((rows, group, lane), lambda i: (0, i, 0)),
    ]
    args = [wt, g2, block]
    aliases = {}
    kernel = y_kernel
    if before is not None:
        specs.append(pl.BlockSpec(memory_space=pl.ANY))
        args.append(before)
        aliases = {3: 0}

        def kernel(w, g, m, unused, *rest):
            y_kernel(w, g, m, *rest)

    return pl.pallas_call(
        kernel,
        grid=(steps,),
        in_specs=specs,
        out_specs=pl.BlockSpec((rows, group, lane), lambda i: (0, part * steps + i, 0)),
        out_shape=jax.ShapeDtypeStruct((rows, 4 * mus, lane), BF),
        input_output_aliases=aliases,
        compiler_params=pltpu.CompilerParams(vmem_limit_bytes=VMEM),
        cost_estimate=pl.CostEstimate(flops=40 * rows * rows * mus * lane, bytes_accessed=80 * rows * mus * lane, transcendentals=0),
        name="y_part",
    )(*args)


def after(value, *others, weight=0):
    return pl.pallas_call(
        lambda *refs: None,
        in_specs=[pl.BlockSpec(memory_space=pl.ANY)] * (1 + len(others)),
        out_specs=pl.BlockSpec(memory_space=pl.ANY),
        out_shape=jax.ShapeDtypeStruct(value.shape, value.dtype),
        input_output_aliases={0: 0},
        compiler_params=pltpu.CompilerParams(vmem_limit_bytes=VMEM),
        cost_estimate=pl.CostEstimate(
            flops=weight * 1000000000, bytes_accessed=weight * 3000000, transcendentals=0
        ),
        name="after",
    )(value, *others)


def contract_kernel(counts, more, tab_ref, *refs):
    out_ref = refs[-1]
    pieces = sum(counts)
    q = refs[0].shape[0]

    @pl.when(pl.program_id(0) == 0)
    def _():
        out_ref[...] = refs[-2][...] if more else jnp.zeros_like(out_ref)

    acc = out_ref[...]
    place = 0
    for source, count in enumerate(counts):
        f_ref = refs[pieces + source]
        for piece in range(count):
            y_ref = refs[place]
            place += 1
            for i in range(0, q, 2):
                lhs = jnp.concatenate([y_ref[i], y_ref[i + 1]], axis=1)
                rhs = jnp.concatenate([f_ref[piece * q + i], f_ref[piece * q + i + 1]], axis=1)
                acc += lax.dot_general(lhs, rhs, (((1,), (1,)), ((), ())), preferred_element_type=F32)
    out_ref[...] = acc


def contract(before, ys, table, chunks, q, steps=2):
    values = [value for value, _ in chunks]
    counts = [value.shape[0] // q // steps for value in values]
    per = sum(counts)
    rows, lane = ys.shape[1], ys.shape[2]
    nus = values[0].shape[1]

    def y_spec(start, count):
        return pl.BlockSpec((q, rows, lane), lambda i, tab: (tab[start + i * count], 0, 0))

    specs = [
        y_spec(start + piece, count)
        for (_, start), count in zip(chunks, counts)
        for piece in range(count)
    ]
    specs += [pl.BlockSpec((count * q, nus, lane), lambda i, tab: (i, 0, 0)) for count in counts]
    args = [table] + [ys] * per + values
    if before is not None:
        specs.append(pl.BlockSpec((rows, nus), lambda i, tab: (0, 0)))
        args.append(before)
    return pl.pallas_call(
        lambda *refs: contract_kernel(counts, before is not None, *refs),
        grid_spec=pltpu.PrefetchScalarGridSpec(
            num_scalar_prefetch=1,
            grid=(steps,),
            in_specs=specs,
            out_specs=pl.BlockSpec((rows, nus), lambda i, tab: (0, 0)),
        ),
        out_shape=jax.ShapeDtypeStruct((rows, nus), F32),
        compiler_params=pltpu.CompilerParams(vmem_limit_bytes=VMEM),
        cost_estimate=pl.CostEstimate(
            flops=2 * rows * nus * lane * q * per * steps,
            bytes_accessed=2 * q * per * steps * lane * (rows + nus),
            transcendentals=0,
        ),
        name="contract",
    )(*args)


def pick(buffer, table, count, others):
    block = (1,) + buffer.shape[1:]
    zeros = (0,) * (buffer.ndim - 1)

    def spec(i):
        return pl.BlockSpec(block, lambda j, tab: (tab[i],) + zeros)

    def kernel(tab_ref, *refs):
        for i in range(count):
            refs[-1][i] = refs[i][0]

    return pl.pallas_call(
        kernel,
        grid_spec=pltpu.PrefetchScalarGridSpec(
            num_scalar_prefetch=1,
            grid=(1,),
            in_specs=[spec(i) for i in range(count)] + [pl.BlockSpec(memory_space=pl.ANY)] * len(others),
            out_specs=pl.BlockSpec((count,) + buffer.shape[1:], lambda j, tab: (0,) + zeros),
        ),
        out_shape=jax.ShapeDtypeStruct((count,) + buffer.shape[1:], buffer.dtype),
        compiler_params=pltpu.CompilerParams(vmem_limit_bytes=VMEM),
        cost_estimate=pl.CostEstimate(flops=1000, bytes_accessed=1000, transcendentals=0),
        name="pick",
    )(table, *([buffer] * count), *others)


def masked_rows(value, half, mask):
    groups = mask.shape[0]
    steps = 2
    rows = value.shape[0] // 2
    step_rows = rows // steps
    table = jnp.concatenate([half.reshape(1), mask]).astype(jnp.int32)
    block = (step_rows,) + value.shape[1:]

    def kernel(tab_ref, in_ref, out_ref):
        row = tab_ref[0] * rows + pl.program_id(0) * step_rows
        keep = tab_ref[1 + row // (value.shape[0] // groups)].astype(F32)
        out_ref[...] = (in_ref[...].astype(F32) * keep).astype(BF)

    return pl.pallas_call(
        kernel,
        grid_spec=pltpu.PrefetchScalarGridSpec(
            num_scalar_prefetch=1,
            grid=(steps,),
            in_specs=[pl.BlockSpec(block, lambda i, tab: (tab[0] * steps + i, 0, 0))],
            out_specs=pl.BlockSpec(block, lambda i, tab: (i, 0, 0)),
        ),
        out_shape=jax.ShapeDtypeStruct((rows,) + value.shape[1:], BF),
        compiler_params=pltpu.CompilerParams(vmem_limit_bytes=VMEM),
        cost_estimate=pl.CostEstimate(flops=1000, bytes_accessed=1000, transcendentals=0),
        name="masked_rows",
    )(table, value)


def g_kernel(tab_ref, own_ref, oth_ref, out_ref):
    tile = tab_ref[pl.program_id(0)]
    mine = tile // 2 == tab_ref[3]
    g = jnp.where(mine, own_ref[...].astype(F32), oth_ref[...].astype(F32)).astype(BF)
    n = g.shape[0]
    out_ref[...] = jnp.zeros_like(out_ref)
    out_ref[0, :n, :n] = g
    out_ref[0, n:, n:] = g


def g_pairs(own, other, table, width):
    def spec():
        return pl.BlockSpec((width, width), lambda i, tab: (tab[i] % 2, tab[2]))

    return pl.pallas_call(
        g_kernel,
        grid_spec=pltpu.PrefetchScalarGridSpec(
            num_scalar_prefetch=1,
            grid=(2,),
            in_specs=[spec(), spec()],
            out_specs=pl.BlockSpec((1, 2 * width, 2 * width), lambda i, tab: (i, 0, 0)),
        ),
        out_shape=jax.ShapeDtypeStruct((2, 2 * width, 2 * width), BF),
        compiler_params=pltpu.CompilerParams(vmem_limit_bytes=VMEM),
        cost_estimate=pl.CostEstimate(flops=1000, bytes_accessed=1000, transcendentals=0),
        name="g_pairs",
    )(table, own, other)


def body(
    coulomb_band, band_mask, dielectric, three_centre, centre_mask, greens, tile_map, batch_order
):
    rows = coulomb_band.shape[0]
    mus = three_centre.shape[1]
    width = three_centre.shape[2]
    z, x, c = lax.axis_index("z"), lax.axis_index("x"), lax.axis_index("core")
    s, h = lax.axis_index("sec"), lax.axis_index("ao")
    ri = (z * NX + x) * NC + c
    tiles = tile_map[:, 0]
    keep = jnp.repeat(centre_mask, rows // centre_mask.shape[0]).astype(BF)

    owners = batch_order[:, :4]
    own_owners = jnp.sum(jnp.where((jnp.arange(2) == s)[:, None], owners, 0), axis=0)
    wanted = jnp.concatenate([jnp.stack([ri, ri + 1 - 2 * c]).astype(jnp.int32), own_owners])
    all_places = jnp.arange(tiles.shape[0], dtype=jnp.int32)
    found = jnp.sum(jnp.where(wanted[:, None] == all_places[None, :], tiles[None, :], 0), axis=1)
    mine = jnp.arange(4, dtype=jnp.int32) == 2 * h + c
    my_tile = jnp.sum(jnp.where(mine, found[2:], 0)).reshape(1)
    ds, dh = jnp.array([0, 0, 1, 1] * 2), jnp.array([0, 1, 0, 1] * 2)
    to_core = jnp.array([1] * 4 + [0] * 4)
    flow = (s ^ ds) * 4 + (h ^ dh) * 2 + (c ^ to_core)
    flow_owner = jnp.sum(
        jnp.where(flow[:, None] == jnp.arange(8)[None, :], owners.reshape(1, -1), 0), axis=1
    ).astype(jnp.int32)
    table = flow_owner // NC
    here_now = (flow_owner[4:] % NC == c)[:, None, None, None]

    send = masked_rows(three_centre, h, centre_mask)
    own_x = after(dielectric[0], send)
    ring = [(i, (i + 1) % (CHIPS * NC)) for i in range(CHIPS * NC)]
    back = [(j, i) for i, j in ring]
    before = lax.ppermute(own_x, ("z", "x", "core"), ring)
    behind = lax.ppermute(own_x, ("z", "x", "core"), back)
    g_other = shift(greens[0], "ao", 1)
    mask_full = jnp.repeat(jnp.repeat(band_mask, 64, axis=0), 64, axis=1).astype(BF)
    band = coulomb_band * mask_full
    stacked = jnp.concatenate([before, own_x, behind], axis=0)
    wt = lax.dot_general(stacked, band, (((0,), (1,)), ((), ())), preferred_element_type=F32).astype(BF)
    wt = wt * keep[None, :]
    wt = wt.reshape(2, rows, rows)
    half_rows = rows // 2
    q = half_rows // CHIPS
    wt_own = jnp.where(c == 0, wt[0], wt[1])
    wt_oth = shift(jnp.where(c == 0, wt[1], wt[0]), "core", 1)
    g2 = g_pairs(
        greens[0], g_other, jnp.concatenate([found[:2], my_tile, h.reshape(1)]).astype(jnp.int32), width
    )

    m_core = after(shift(three_centre, "core", 1), g_other)
    m_both = lax.ppermute(m_core, ("sec", "core", "ao"), along_y())

    send = after(send, before, behind)
    spread = lax.all_to_all(send, ("z", "x"), 0, 0, tiled=True).reshape(CHIPS, q, mus, width)
    picked = pick(spread, table, 8, (m_both,))
    m_both = after(m_both, picked)
    m_sec = shift(m_both, "core", 1)
    ys_0 = y_part(None, 0, after(wt_own, picked), g2, three_centre)
    given = shift(picked[:4], "core", 1)
    pieces = jnp.where(here_now, picked[4:], given)
    got = [
        pieces[0],
        shift(pieces[1], "ao", 1),
        shift(pieces[2], "sec", 1),
        lax.ppermute(pieces[3], ("sec", "ao"), [(i, 3 - i) for i in range(4)]),
    ]
    got = jnp.stack(got).reshape(2, 2, q, mus, width)
    got = jnp.where(s == 0, got, got[::-1])
    got = jnp.where(h == 0, got, got[:, ::-1])
    halves = jnp.transpose(got, (1, 2, 0, 3, 4)).reshape(2, q, 2 * mus, width)
    piece_a, piece_b = halves[0], after(halves[1], ys_0)
    ys_1 = y_part(ys_0, 1, wt_oth, g2, m_core)
    ys_2 = y_part(ys_1, 3, wt_oth, g2, m_both)
    ys = y_part(ys_2, 2, wt_own, g2, m_sec)

    rel_z = [0]
    for step in range(1, NZ // 2):
        rel_z += [step, -step]
    rel_z.append(NZ // 2)
    lists = [], [], []

    def ids(first, zs, xs):
        start = len(lists[0])
        for dz in zs:
            for dx in xs:
                for entry, item in zip(lists, (first, dz, dx)):
                    entry.append(item)
        return start

    def ids_a(offset, first, count):
        return ids(0, [offset], list(range(first, first + count)))

    def ids_b(offset, first, count):
        return ids(CHIPS, rel_z[first : first + count], [offset])

    a_ids = {off: ids_a(off, 0, NX) for off in rel_z[:-1]}
    a_ids[4, 0], a_ids[4, 2] = ids_a(4, 0, 2), ids_a(4, 2, 2)
    b_ids = {off: ids_b(off, 0, NZ) for off in (0, 1, -1)}
    b_ids[2, 0], b_ids[2, 4] = ids_b(2, 0, 4), ids_b(2, 4, 4)
    first, off_z, off_x = (jnp.array(entry, jnp.int32) for entry in lists)
    places = first + ((z - off_z) % NZ) * NX + (x - off_x) % NX

    up, down = shift(piece_b, "z", 1), shift(piece_b, "z", -1)
    up, down = after(up, ys_1), after(down, ys_1)
    pieces = [piece_b, up, down]
    piece_a = after(piece_a, up, down)
    chunk_a = jnp.concatenate([piece_a] + [shift(piece_a, "x", d) for d in range(1, NX)], axis=0)
    up, down = shift(up, "z", 1), shift(down, "z", -1)
    pieces += [up, down]
    up, down = shift(up, "z", 1), shift(down, "z", -1)
    pieces += [up, down]
    pieces.append(shift(up, "z", 1))
    chunk_b = jnp.concatenate(pieces, axis=0)
    chunk_a = after(chunk_a, chunk_b)

    up1, down1 = shift(chunk_a, "z", 1), shift(chunk_a, "z", -1)
    up1, down1 = after(up1, ys_2), after(down1, ys_2)
    up_b, down_b = shift(chunk_b, "x", 1), shift(chunk_b, "x", -1)
    up2, down2 = shift(up1, "z", 1), shift(down1, "z", -1)
    up2, down2 = after(up2, ys), after(down2, ys)
    up3, down3 = shift(up2, "z", 1), shift(down2, "z", -1)
    total = contract(
        None,
        ys,
        places,
        [
            (chunk_a, a_ids[0]),
            (chunk_b, b_ids[0]),
        ],
        q,
    )
    up3, down3 = after(up3, total), after(down3, total)
    part = chunk_a.shape[0] // 2
    last_up, last_down = shift(up3[:part], "z", 1), shift(down3[part:], "z", -1)
    part_b = chunk_b.shape[0] // 2
    last_up_b, last_down_b = shift(up_b[:part_b], "x", 1), shift(down_b[part_b:], "x", -1)
    total = contract(
        total,
        ys,
        places,
        [
            (up1, a_ids[1]),
            (down1, a_ids[-1]),
            (up2, a_ids[2]),
            (down2, a_ids[-2]),
            (up3, a_ids[3]),
            (down3, a_ids[-3]),
            (up_b, b_ids[1]),
            (down_b, b_ids[-1]),
            (last_up_b, b_ids[2, 0]),
            (last_down_b, b_ids[2, 4]),
        ],
        q,
    )
    total = contract(total, ys, places, [(last_up, a_ids[4, 0]), (last_down, a_ids[4, 2])], q)

    row_places = jnp.arange(8, dtype=jnp.int32)
    starts = 2 * jnp.concatenate([found[:2], found[:2]]) + jnp.stack([s, s, 1 - s, 1 - s])
    here = starts[:, None] == row_places[None, :]
    partial = jnp.sum(jnp.where(here[:, :, None, None], total.reshape(4, 1, mus, width), 0.0), axis=0)
    partial = partial.reshape(8 * mus, width)
    moved = lax.all_to_all(partial, ("z", "x", "core", "ao"), 0, 0, tiled=True)
    own_rows = partial.shape[0] // (CHIPS * NC * 2)
    summed = jnp.sum(moved.reshape(CHIPS, NC, 2, own_rows, width), axis=0)
    col_places = jnp.arange(4, dtype=jnp.int32)
    there = found[2:].reshape(2, NC).T[:, :, None] == col_places
    out = -jnp.sum(jnp.where(there[:, :, None, :, None], summed[:, :, :, None, :], 0.0), axis=(0, 1))
    return out.reshape(1, own_rows, 4 * width)


def solution(mesh):
    devices = mesh.devices.reshape(2, NZ, NX, NC, 2)
    split = Mesh(devices, ("sec", "z", "x", "core", "ao"))
    ri = ("z", "x", "core")
    placed = (
        P(ri, None),
        P(ri, None),
        P("sec", ri, "ao"),
        P(ri, "sec", None),
        P(ri),
        P("sec", "ao", None),
        P(),
        P(),
    )
    return jax.shard_map(
        body, mesh=split, in_specs=placed, out_specs=P("sec", ri + ("ao",), None), check_vma=False
    )
```
